1024 devices in a mesh: grp: 32 (over y, z_hi, x), en: 32 (over z_lo, core).
Axes of the slice: x: 4, y: 4, z: 32 (z_hi: 2, z_lo: 16; z = z_hi * 16 + z_lo), core: 2. Of those that a mesh axis runs over, the one named last changes fastest.
Arguments:
- lesser: float32 [2, 16384, 4096], P(None, 'grp', 'en'), may hold values from -6 to 6
- greater: float32 [2, 16384, 4096], P(None, 'grp', 'en'), may hold values from -6 to 6
- mirror: int32 [16384], P('grp'), may hold values from 0 to 16383, as said below
Outputs:
- polar: float32 [2, 16384, 4096], P(None, 'grp', 'en')
The draws below stay inside these ranges and needn't reach their ends.
Inputs may be any that keep to these rules, and one draw needn't show every extreme that they name: mirror is an involution without fixed points; for every entry p, mirror[p] // 16 = (p // 16 + 16384 // 32) mod (1024), so the mirrored entry lies in the aligned block of 16 entries 16384 / 2 entries away.
All inputs are finite; a program needn't handle non-finite values.
Results may differ from the reference program's by a relative error of at most 0.000098.
Values sent between devices are 32-bit elements; how exact they have to be, the bound alone decides.
A program may use at most 32 MiB of HBM per device.

```python
import jax
import jax.numpy as jnp
from jax import lax

NE = 4096
EN_DEV = 16
NPG = 512
NP = 16384
N_GRP = 32


def draw_mirror(key, part):
    blocks = NP // EN_DEV
    half = blocks // 2
    subkeys = jax.random.split(jax.random.fold_in(key, 7), half)
    orders = jax.vmap(lambda sub: jax.random.permutation(sub, EN_DEV))(subkeys).astype(jnp.int32)
    base = jnp.arange(half, dtype=jnp.int32)[:, None] * EN_DEV
    upper = base + half * EN_DEV + orders
    lower = base + jnp.argsort(orders, axis=1, stable=True).astype(jnp.int32)
    return jnp.concatenate([upper.reshape(-1), lower.reshape(-1)]).astype(jnp.int32)


def shard_levels(stream_key, dims, shards, least, high):
    def one(dim, parts):
        heights = jax.random.uniform(jax.random.fold_in(jax.random.fold_in(stream_key, 6), dim), (parts,), jnp.float32, least / len(shards), high / len(shards))
        return jnp.repeat(jnp.exp(heights), dims[dim] // parts).reshape((-1,) + (1,) * (len(dims) - dim - 1))

    factor_of = one(*shards[0])
    for cut in shards[1:]:
        factor_of = factor_of * one(*cut)
    return factor_of


def noise(stream_key, extent, spread, reach, cuts=(), kind=jnp.bfloat16):
    array = spread * jax.random.normal(stream_key, extent, jnp.float32)
    if cuts:
        array = array * shard_levels(stream_key, extent, cuts, -0.22, 0.18)
    return jnp.clip(array, -reach, reach).astype(kind)


def setup_inputs(seed: int = 0) -> dict:
    streams_of = jax.random.split(jax.random.key(seed), 4)
    return {
        "lesser": noise(streams_of[0], (2, NP, NE), 1.0, 6.0, ((1, 32), (2, 32)), jnp.float32),
        "greater": noise(streams_of[1], (2, NP, NE), 1.0, 6.0, ((1, 32), (2, 32)), jnp.float32),
        "mirror": draw_mirror(jax.random.fold_in(streams_of[3], 71), 0),
    }


def reference(lesser, greater, mirror):
    def one_group(start):
        rows_lesser = lax.dynamic_slice_in_dim(lesser, start, NPG, 1)
        partner = lax.dynamic_slice_in_dim(mirror, start, NPG, 0)
        rows_greater = jnp.take(greater, partner, axis=1)
        left = lax.complex(rows_lesser[0], rows_lesser[1])
        right = lax.complex(rows_greater[0], rows_greater[1])
        spectrum = jnp.fft.fft(left, axis=1) * (jnp.fft.ifft(right, axis=1) * NE)
        correl = jnp.fft.ifft(spectrum, axis=1)
        factor = NE ** -0.5
        return jnp.stack([jnp.imag(correl) * factor, -jnp.real(correl) * factor])

    starts = (jnp.arange(N_GRP) * NPG).astype(jnp.int32)
    blocks = lax.map(one_group, starts)
    return jnp.transpose(blocks, (1, 0, 2, 3)).reshape(2, NP, NE)
```

```python
import functools
import math

import jax
import jax.numpy as jnp
import numpy as np
from jax import lax
from jax.experimental import pallas as pl
from jax.experimental.pallas import tpu as pltpu
from jax.sharding import PartitionSpec as P

MESH = pl.DeviceIdType.MESH
RADIX = 32
LANES = 128
SUB = 8


def tables():
    length = RADIX * LANES
    lane = np.arange(LANES)
    angle = 2.0 * math.pi / LANES * (lane[:, None] * lane[None, :] % LANES)
    cos, sin = np.cos(angle), np.sin(angle)
    lane_table = np.block([[cos, sin], [-sin, cos]]).astype(np.float32)
    series = np.arange(RADIX)
    twist = 2.0 * math.pi / length * (series[:, None] * lane[None, :] % length)
    twist_table = np.stack([np.cos(twist), np.sin(twist)]).astype(np.float32)
    return lane_table, twist_table


def times(value, turn):
    re, im = value
    c, s = math.cos(turn), math.sin(turn)
    return re * c - im * s, re * s + im * c


def add(left, right):
    return left[0] + right[0], left[1] + right[1]


def sub(left, right):
    return left[0] - right[0], left[1] - right[1]


def quarter(value):
    return -value[1], value[0]


def dft4(x):
    s02, d02 = add(x[0], x[2]), sub(x[0], x[2])
    s13, d13 = add(x[1], x[3]), quarter(sub(x[1], x[3]))
    return [add(s02, s13), add(d02, d13), sub(s02, s13), sub(d02, d13)]


def dft8(x):
    even, odd = dft4(x[0::2]), dft4(x[1::2])
    root = math.sqrt(0.5)
    r1, i1 = odd[1]
    odd[1] = ((r1 - i1) * root, (r1 + i1) * root)
    odd[2] = quarter(odd[2])
    r3, i3 = odd[3]
    odd[3] = ((-r3 - i3) * root, (r3 - i3) * root)
    return [add(e, o) for e, o in zip(even, odd)] + [sub(e, o) for e, o in zip(even, odd)]


def dft32(load, mid, store):
    for j in range(8):
        four = dft4([load(8 * i + j) for i in range(4)])
        for q in range(4):
            value = four[q] if j * q == 0 else times(four[q], 2.0 * math.pi * j * q / RADIX)
            mid[q * 8 + j, :, 0:LANES] = value[0]
            mid[q * 8 + j, :, LANES : 2 * LANES] = value[1]
    for q in range(4):
        eight = dft8(
            [(mid[q * 8 + j, :, 0:LANES], mid[q * 8 + j, :, LANES : 2 * LANES]) for j in range(8)]
        )
        for m in range(8):
            store(q + 4 * m, eight[m])


def forward(load, twist, lane_table, mid, work):
    def store(k, value):
        re, im = value
        c, s = twist[0, pl.ds(k, 1), :], twist[1, pl.ds(k, 1), :]
        work[k, :, 0:LANES] = re * c - im * s
        work[k, :, LANES : 2 * LANES] = re * s + im * c

    dft32(load, mid, store)
    return lanes(work, lane_table)


def lanes(work, lane_table):
    rows = work[...].reshape(RADIX * SUB, 2 * LANES)
    out = jnp.dot(
        rows, lane_table[...], precision=lax.Precision.HIGHEST, preferred_element_type=jnp.float32
    )
    return out.reshape(RADIX, SUB, 2 * LANES)


def inverse(twist, lane_table, mid, work, store):
    work[...] = lanes(work, lane_table)

    def load(k):
        re, im = work[k, :, 0:LANES], work[k, :, LANES : 2 * LANES]
        c, s = twist[0, pl.ds(k, 1), :], twist[1, pl.ds(k, 1), :]
        return re * c - im * s, re * s + im * c

    dft32(load, mid, store)


def kernel(
    n_grp, n_en, rows,
    lesser, greater, mirror, lane_hbm, twist_hbm, out,
    recv_b, recv_a, c_buf, lane_table, twist, spec_b, perm_b, mid, work,
    send_sem, recv_sem, local_sem, self_sem,
):
    me_g, me_e = lax.axis_index("grp"), lax.axis_index("en")
    partner = lax.rem(me_g + n_grp // 2, n_grp)
    parts = rows // SUB

    barrier = pltpu.get_barrier_semaphore()

    def greet(step, carry):
        other = lax.rem(me_e + step, n_en)

        @pl.when(step > 0)
        def _():
            pl.semaphore_signal(barrier, inc=1, device_id=(me_g, other), device_id_type=MESH)

        pl.semaphore_signal(barrier, inc=1, device_id=(partner, other), device_id_type=MESH)
        return carry

    lax.fori_loop(0, n_en, greet, 0)
    pl.semaphore_wait(barrier, 2 * n_en - 1)

    def send_b(step, carry):
        other = lax.rem(me_e + n_en // 2 + step, n_en)
        pltpu.make_async_remote_copy(
            src_ref=greater.at[:, pl.ds(pl.multiple_of(other * rows, rows), rows), :],
            dst_ref=recv_b.at[me_e],
            send_sem=send_sem.at[0],
            recv_sem=recv_sem.at[0],
            device_id=(partner, other),
            device_id_type=MESH,
        ).start()
        return carry

    lax.fori_loop(0, n_en, send_b, 0)

    def order(step):
        hop = jnp.where(step % 2 == 0, n_en // 2 + step // 2, n_en // 2 - 1 - step // 2)
        return lax.rem(me_e + hop, n_en)

    for part in range(parts):

        def send_a(step, carry, part=part):
            other = order(step)
            pltpu.make_async_remote_copy(
                src_ref=lesser.at[
                    :, pl.ds(pl.multiple_of(other * rows + part * SUB, SUB), SUB), :
                ],
                dst_ref=recv_a.at[part, me_e],
                send_sem=send_sem.at[1 + part],
                recv_sem=recv_sem.at[1 + part],
                device_id=(me_g, other),
                device_id_type=MESH,
            ).start()
            return carry

        lax.fori_loop(0, n_en - 1, send_a, 0)

    def own(part):
        return pltpu.make_async_copy(
            lesser.at[:, pl.ds(pl.multiple_of(me_e * rows + part * SUB, SUB), SUB), :],
            recv_a.at[part, me_e],
            self_sem.at[part],
        )

    load_lane = pltpu.make_async_copy(lane_hbm, lane_table, local_sem.at[0])
    load_twist = pltpu.make_async_copy(twist_hbm, twist, local_sem.at[1])
    load_lane.start()
    load_twist.start()
    for part in range(parts):
        own(part).start()
    load_lane.wait()
    load_twist.wait()

    def await_recv(ref, sem):
        pltpu.make_async_copy(ref, ref, sem).wait()

    await_recv(recv_b, recv_sem.at[0])
    for part in range(parts):
        spec_b[:, part * SUB : (part + 1) * SUB, :] = forward(
            lambda d, part=part: (
                recv_b[d, 0, part * SUB : (part + 1) * SUB, :],
                recv_b[d, 1, part * SUB : (part + 1) * SUB, :],
            ),
            twist, lane_table, mid, work,
        )
    for row in range(rows):
        pick = lax.rem(mirror[me_e * rows + row], rows)
        perm_b[:, row : row + 1, :] = spec_b[:, pl.ds(pick, 1), :]

    scale = float(RADIX * LANES) ** -1.5
    for part in range(parts):
        own(part).wait()
        await_recv(recv_a.at[part, pl.ds(0, n_en - 1)], recv_sem.at[1 + part])
        spec = forward(
            lambda d, part=part: (recv_a[part, d, 1], recv_a[part, d, 0]),
            twist, lane_table, mid, work,
        )
        left_re, left_im = spec[:, :, 0:LANES], spec[:, :, LANES : 2 * LANES]
        block = perm_b[:, part * SUB : (part + 1) * SUB, :]
        right_re, right_im = block[:, :, 0:LANES], block[:, :, LANES : 2 * LANES]
        work[:, :, 0:LANES] = (left_re * right_re + left_im * right_im) * scale
        work[:, :, LANES : 2 * LANES] = (left_re * right_im - left_im * right_re) * scale

        def store(d, value, part=part):
            c_buf[part, d, 0] = value[0]
            c_buf[part, d, 1] = value[1]

        inverse(twist, lane_table, mid, work, store)

        place = pl.ds(pl.multiple_of(me_e * rows + part * SUB, SUB), SUB)

        def send_c(step, carry, part=part, place=place):
            other = order(step)
            pltpu.make_async_remote_copy(
                src_ref=c_buf.at[part, other],
                dst_ref=out.at[:, place, :],
                send_sem=send_sem.at[1 + parts + part],
                recv_sem=recv_sem.at[1 + parts],
                device_id=(me_g, other),
                device_id_type=MESH,
            ).start()
            return carry

        lax.fori_loop(0, n_en - 1, send_c, 0)
        pltpu.make_async_copy(
            c_buf.at[part, me_e], out.at[:, place, :], self_sem.at[parts + part]
        ).start()

    for part in range(parts):
        place = pl.ds(pl.multiple_of(me_e * rows + part * SUB, SUB), SUB)
        pltpu.make_async_copy(
            c_buf.at[part, me_e], out.at[:, place, :], self_sem.at[parts + part]
        ).wait()
    await_recv(recv_b, send_sem.at[0])
    for part in range(parts):
        await_recv(recv_a.at[part, pl.ds(0, n_en - 1)], send_sem.at[1 + part])
        await_recv(c_buf.at[part, pl.ds(0, n_en - 1)], send_sem.at[1 + parts + part])
    length = rows * (n_en - 1)
    await_recv(out.at[:, pl.ds(0, length), :], recv_sem.at[1 + parts])


def body(lesser, greater, mirror):
    n_grp, n_en = lax.axis_size("grp"), lax.axis_size("en")
    rows = lesser.shape[1] // n_en
    parts = rows // SUB
    lane_table, twist_table = tables()
    wide = (RADIX, SUB, 2 * LANES)
    f32 = jnp.float32
    return pl.pallas_call(
        functools.partial(kernel, n_grp, n_en, rows),
        out_shape=jax.ShapeDtypeStruct(lesser.shape, f32),
        in_specs=[
            pl.BlockSpec(memory_space=pl.ANY),
            pl.BlockSpec(memory_space=pl.ANY),
            pl.BlockSpec(memory_space=pltpu.SMEM),
            pl.BlockSpec(memory_space=pl.ANY),
            pl.BlockSpec(memory_space=pl.ANY),
        ],
        out_specs=pl.BlockSpec(memory_space=pl.ANY),
        scratch_shapes=[
            pltpu.VMEM((n_en, 2, rows, LANES), f32),
            pltpu.VMEM((parts, n_en, 2, SUB, LANES), f32),
            pltpu.VMEM((parts, n_en, 2, SUB, LANES), f32),
            pltpu.VMEM(lane_table.shape, f32),
            pltpu.VMEM(twist_table.shape, f32),
            pltpu.VMEM((RADIX, rows, 2 * LANES), f32),
            pltpu.VMEM((RADIX, rows, 2 * LANES), f32),
            pltpu.VMEM(wide, f32),
            pltpu.VMEM(wide, f32),
            pltpu.SemaphoreType.DMA((1 + 2 * parts,)),
            pltpu.SemaphoreType.DMA((2 + parts,)),
            pltpu.SemaphoreType.DMA((2,)),
            pltpu.SemaphoreType.DMA((2 * parts,)),
        ],
        compiler_params=pltpu.CompilerParams(
            collective_id=0, has_side_effects=True, vmem_limit_bytes=60 * 1024 * 1024
        ),
    )(lesser, greater, mirror, jnp.asarray(lane_table), jnp.asarray(twist_table))


def solution(mesh):
    in_specs = (P(None, "grp", "en"), P(None, "grp", "en"), P("grp"))
    out_specs = P(None, "grp", "en")
    return jax.shard_map(body, mesh=mesh, in_specs=in_specs, out_specs=out_specs, check_vma=False)
```

```python
import functools
import math

import jax
import jax.numpy as jnp
import numpy as np
from jax import lax
from jax.experimental import pallas as pl
from jax.experimental.pallas import tpu as pltpu
from jax.sharding import PartitionSpec as P

MESH = pl.DeviceIdType.MESH
RADIX = 32
LANES = 128
SUB = 8
CORES = 2


def tables():
    length = RADIX * LANES
    lane = np.arange(LANES)
    angle = 2.0 * math.pi / LANES * (lane[:, None] * lane[None, :] % LANES)
    cos, sin = np.cos(angle), np.sin(angle)
    lane_table = np.block([[cos, sin], [-sin, cos]]).astype(np.float32)
    series = np.arange(RADIX)
    twist = 2.0 * math.pi / length * (series[:, None] * lane[None, :] % length)
    twist_table = np.stack([np.cos(twist), np.sin(twist)]).astype(np.float32)
    return lane_table, twist_table


def times(value, turn):
    re, im = value
    c, s = math.cos(turn), math.sin(turn)
    return re * c - im * s, re * s + im * c


def add(left, right):
    return left[0] + right[0], left[1] + right[1]


def sub(left, right):
    return left[0] - right[0], left[1] - right[1]


def quarter(value):
    return -value[1], value[0]


def dft4(x):
    s02, d02 = add(x[0], x[2]), sub(x[0], x[2])
    s13, d13 = add(x[1], x[3]), quarter(sub(x[1], x[3]))
    return [add(s02, s13), add(d02, d13), sub(s02, s13), sub(d02, d13)]


def dft8(x):
    even, odd = dft4(x[0::2]), dft4(x[1::2])
    root = math.sqrt(0.5)
    r1, i1 = odd[1]
    odd[1] = ((r1 - i1) * root, (r1 + i1) * root)
    odd[2] = quarter(odd[2])
    r3, i3 = odd[3]
    odd[3] = ((-r3 - i3) * root, (r3 - i3) * root)
    return [add(e, o) for e, o in zip(even, odd)] + [sub(e, o) for e, o in zip(even, odd)]


def dft32(load, mid, store):
    for j in range(8):
        four = dft4([load(8 * i + j) for i in range(4)])
        for q in range(4):
            value = four[q] if j * q == 0 else times(four[q], 2.0 * math.pi * j * q / RADIX)
            mid[q * 8 + j, :, 0:LANES] = value[0]
            mid[q * 8 + j, :, LANES : 2 * LANES] = value[1]
    for q in range(4):
        eight = dft8(
            [(mid[q * 8 + j, :, 0:LANES], mid[q * 8 + j, :, LANES : 2 * LANES]) for j in range(8)]
        )
        for m in range(8):
            store(q + 4 * m, eight[m])


def forward(load, twist, lane_table, mid, work):
    def store(k, value):
        re, im = value
        c, s = twist[0, pl.ds(k, 1), :], twist[1, pl.ds(k, 1), :]
        work[k, :, 0:LANES] = re * c - im * s
        work[k, :, LANES : 2 * LANES] = re * s + im * c

    dft32(load, mid, store)
    return lanes(work, lane_table)


def lanes(work, lane_table):
    rows = work[...].reshape(RADIX * SUB, 2 * LANES)
    out = jnp.dot(
        rows, lane_table[...], precision=lax.Precision.HIGHEST, preferred_element_type=jnp.float32
    )
    return out.reshape(RADIX, SUB, 2 * LANES)


def inverse(twist, lane_table, mid, work, store):
    work[...] = lanes(work, lane_table)

    def load(k):
        re, im = work[k, :, 0:LANES], work[k, :, LANES : 2 * LANES]
        c, s = twist[0, pl.ds(k, 1), :], twist[1, pl.ds(k, 1), :]
        return re * c - im * s, re * s + im * c

    dft32(load, mid, store)


def kernel(
    n_grp, n_en, rows,
    lesser, greater, mirror, lane_hbm, twist_hbm, out,
    recv_b, recv_a, c_buf, lane_table, twist, spec_b, perm_b, mid, work,
    send_sem, recv_sem, local_sem, self_sem, here_sem, mate_sem,
):
    me_g, me_e = lax.axis_index("grp"), lax.axis_index("en")
    partner = lax.rem(me_g + n_grp // 2, n_grp)
    parts = rows // SUB

    chips = n_en // CORES
    late = jnp.where(lax.rem(me_g, n_grp // 2) == 0, chips - 4, 0)
    me_z = me_e // CORES
    rank = jnp.where(me_z == 0, late, me_z - (me_z <= late).astype(jnp.int32))

    def chip_of(place):
        return jnp.where(place == late, 0, place + (place < late).astype(jnp.int32))

    core = lax.rem(me_e, CORES)
    mates = [(me_g, me_e + 1 - 2 * core), (partner, me_z * CORES), (partner, me_z * CORES + 1)]

    def signal(sem, device):
        pl.semaphore_signal(sem, inc=1, device_id=device, device_id_type=MESH)

    barrier = pltpu.get_barrier_semaphore()
    for mate in mates:
        signal(barrier, mate)

    def greet(place, carry):
        signal(barrier, (me_g, chip_of(place) * CORES + core))
        return carry

    lax.fori_loop(rank + 1, chips, greet, 0)
    pl.semaphore_wait(barrier, rank + len(mates))
    for mate in mates:
        signal(mate_sem, mate)

    def announce(place, carry):
        signal(here_sem.at[rank], (me_g, chip_of(place) * CORES + core))
        return carry

    lax.fori_loop(0, rank, announce, 0)
    pl.semaphore_wait(mate_sem, len(mates))

    def send_b(chip):
        for core in range(CORES):
            other = chip * CORES + core
            pltpu.make_async_remote_copy(
                src_ref=greater.at[:, pl.ds(pl.multiple_of(other * rows, rows), rows), :],
                dst_ref=recv_b.at[me_e],
                send_sem=send_sem.at[0],
                recv_sem=recv_sem.at[0],
                device_id=(partner, other),
                device_id_type=MESH,
            ).start()

    def send_b_below(step, carry):
        send_b(chip_of(lax.rem(rank + chips // 2 + step, rank + 1)))
        return carry

    lax.fori_loop(0, rank + 1, send_b_below, 0)

    def send_b_above(place, carry):
        pl.semaphore_wait(here_sem.at[place], 1)
        send_b(chip_of(place))
        return carry

    lax.fori_loop(rank + 1, chips, send_b_above, 0)

    def order(step):
        hop = jnp.where(step % 2 == 0, n_en // 2 + step // 2, n_en // 2 - 1 - step // 2)
        return lax.rem(me_e + hop, n_en)

    for part in range(parts):

        def send_a(step, carry, part=part):
            other = order(step)
            pltpu.make_async_remote_copy(
                src_ref=lesser.at[
                    :, pl.ds(pl.multiple_of(other * rows + part * SUB, SUB), SUB), :
                ],
                dst_ref=recv_a.at[part, me_e],
                send_sem=send_sem.at[1 + part],
                recv_sem=recv_sem.at[1 + part],
                device_id=(me_g, other),
                device_id_type=MESH,
            ).start()
            return carry

        lax.fori_loop(0, n_en - 1, send_a, 0)

    def own(part):
        return pltpu.make_async_copy(
            lesser.at[:, pl.ds(pl.multiple_of(me_e * rows + part * SUB, SUB), SUB), :],
            recv_a.at[part, me_e],
            self_sem.at[part],
        )

    load_lane = pltpu.make_async_copy(lane_hbm, lane_table, local_sem.at[0])
    load_twist = pltpu.make_async_copy(twist_hbm, twist, local_sem.at[1])
    load_lane.start()
    load_twist.start()
    for part in range(parts):
        own(part).start()
    load_lane.wait()
    load_twist.wait()

    def await_recv(ref, sem):
        pltpu.make_async_copy(ref, ref, sem).wait()

    await_recv(recv_b, recv_sem.at[0])
    for part in range(parts):
        spec_b[:, part * SUB : (part + 1) * SUB, :] = forward(
            lambda d, part=part: (
                recv_b[d, 0, part * SUB : (part + 1) * SUB, :],
                recv_b[d, 1, part * SUB : (part + 1) * SUB, :],
            ),
            twist, lane_table, mid, work,
        )
    for row in range(rows):
        pick = lax.rem(mirror[me_e * rows + row], rows)
        perm_b[:, row : row + 1, :] = spec_b[:, pl.ds(pick, 1), :]

    scale = float(RADIX * LANES) ** -1.5
    for part in range(parts):
        own(part).wait()
        await_recv(recv_a.at[part, pl.ds(0, n_en - 1)], recv_sem.at[1 + part])
        spec = forward(
            lambda d, part=part: (recv_a[part, d, 1], recv_a[part, d, 0]),
            twist, lane_table, mid, work,
        )
        left_re, left_im = spec[:, :, 0:LANES], spec[:, :, LANES : 2 * LANES]
        block = perm_b[:, part * SUB : (part + 1) * SUB, :]
        right_re, right_im = block[:, :, 0:LANES], block[:, :, LANES : 2 * LANES]
        work[:, :, 0:LANES] = (left_re * right_re + left_im * right_im) * scale
        work[:, :, LANES : 2 * LANES] = (left_re * right_im - left_im * right_re) * scale

        def store(d, value, part=part):
            c_buf[part, d, 0] = value[0]
            c_buf[part, d, 1] = value[1]

        inverse(twist, lane_table, mid, work, store)

        place = pl.ds(pl.multiple_of(me_e * rows + part * SUB, SUB), SUB)

        def send_c(step, carry, part=part, place=place):
            other = order(step)
            pltpu.make_async_remote_copy(
                src_ref=c_buf.at[part, other],
                dst_ref=out.at[:, place, :],
                send_sem=send_sem.at[1 + parts + part],
                recv_sem=recv_sem.at[1 + parts],
                device_id=(me_g, other),
                device_id_type=MESH,
            ).start()
            return carry

        lax.fori_loop(0, n_en - 1, send_c, 0)
        pltpu.make_async_copy(
            c_buf.at[part, me_e], out.at[:, place, :], self_sem.at[parts + part]
        ).start()

    for part in range(parts):
        place = pl.ds(pl.multiple_of(me_e * rows + part * SUB, SUB), SUB)
        pltpu.make_async_copy(
            c_buf.at[part, me_e], out.at[:, place, :], self_sem.at[parts + part]
        ).wait()
    await_recv(recv_b, send_sem.at[0])
    for part in range(parts):
        await_recv(recv_a.at[part, pl.ds(0, n_en - 1)], send_sem.at[1 + part])
        await_recv(c_buf.at[part, pl.ds(0, n_en - 1)], send_sem.at[1 + parts + part])
    length = rows * (n_en - 1)
    await_recv(out.at[:, pl.ds(0, length), :], recv_sem.at[1 + parts])


def body(lesser, greater, mirror):
    n_grp, n_en = lax.axis_size("grp"), lax.axis_size("en")
    rows = lesser.shape[1] // n_en
    parts = rows // SUB
    lane_table, twist_table = tables()
    wide = (RADIX, SUB, 2 * LANES)
    f32 = jnp.float32
    return pl.pallas_call(
        functools.partial(kernel, n_grp, n_en, rows),
        out_shape=jax.ShapeDtypeStruct(lesser.shape, f32),
        in_specs=[
            pl.BlockSpec(memory_space=pl.ANY),
            pl.BlockSpec(memory_space=pl.ANY),
            pl.BlockSpec(memory_space=pltpu.SMEM),
            pl.BlockSpec(memory_space=pl.ANY),
            pl.BlockSpec(memory_space=pl.ANY),
        ],
        out_specs=pl.BlockSpec(memory_space=pl.ANY),
        scratch_shapes=[
            pltpu.VMEM((n_en, 2, rows, LANES), f32),
            pltpu.VMEM((parts, n_en, 2, SUB, LANES), f32),
            pltpu.VMEM((parts, n_en, 2, SUB, LANES), f32),
            pltpu.VMEM(lane_table.shape, f32),
            pltpu.VMEM(twist_table.shape, f32),
            pltpu.VMEM((RADIX, rows, 2 * LANES), f32),
            pltpu.VMEM((RADIX, rows, 2 * LANES), f32),
            pltpu.VMEM(wide, f32),
            pltpu.VMEM(wide, f32),
            pltpu.SemaphoreType.DMA((1 + 2 * parts,)),
            pltpu.SemaphoreType.DMA((2 + parts,)),
            pltpu.SemaphoreType.DMA((2,)),
            pltpu.SemaphoreType.DMA((2 * parts,)),
            pltpu.SemaphoreType.REGULAR((n_en // CORES,)),
            pltpu.SemaphoreType.REGULAR,
        ],
        compiler_params=pltpu.CompilerParams(
            collective_id=0, has_side_effects=True, vmem_limit_bytes=60 * 1024 * 1024
        ),
    )(lesser, greater, mirror, jnp.asarray(lane_table), jnp.asarray(twist_table))


def solution(mesh):
    in_specs = (P(None, "grp", "en"), P(None, "grp", "en"), P("grp"))
    out_specs = P(None, "grp", "en")
    return jax.shard_map(body, mesh=mesh, in_specs=in_specs, out_specs=out_specs, check_vma=False)
```

```python
import functools
import math

import jax
import jax.numpy as jnp
import numpy as np
from jax import lax
from jax.experimental import pallas as pl
from jax.experimental.pallas import tpu as pltpu
from jax.sharding import PartitionSpec as P

MESH = pl.DeviceIdType.MESH
RADIX = 32
LANES = 128
SUB = 8
CORES = 2


def tables():
    length = RADIX * LANES
    lane = np.arange(LANES)
    angle = 2.0 * math.pi / LANES * (lane[:, None] * lane[None, :] % LANES)
    cos, sin = np.cos(angle), np.sin(angle)
    lane_table = np.block([[cos, sin], [-sin, cos]]).astype(np.float32)
    series = np.arange(RADIX)
    twist = 2.0 * math.pi / length * (series[:, None] * lane[None, :] % length)
    twist_table = np.stack([np.cos(twist), np.sin(twist)]).astype(np.float32)
    return lane_table, twist_table


def times(value, turn):
    re, im = value
    c, s = math.cos(turn), math.sin(turn)
    return re * c - im * s, re * s + im * c


def add(left, right):
    return left[0] + right[0], left[1] + right[1]


def sub(left, right):
    return left[0] - right[0], left[1] - right[1]


def quarter(value):
    return -value[1], value[0]


def dft4(x):
    s02, d02 = add(x[0], x[2]), sub(x[0], x[2])
    s13, d13 = add(x[1], x[3]), quarter(sub(x[1], x[3]))
    return [add(s02, s13), add(d02, d13), sub(s02, s13), sub(d02, d13)]


def dft8(x):
    even, odd = dft4(x[0::2]), dft4(x[1::2])
    root = math.sqrt(0.5)
    r1, i1 = odd[1]
    odd[1] = ((r1 - i1) * root, (r1 + i1) * root)
    odd[2] = quarter(odd[2])
    r3, i3 = odd[3]
    odd[3] = ((-r3 - i3) * root, (r3 - i3) * root)
    return [add(e, o) for e, o in zip(even, odd)] + [sub(e, o) for e, o in zip(even, odd)]


def dft32(load, mid, store):
    for j in range(8):
        four = dft4([load(8 * i + j) for i in range(4)])
        for q in range(4):
            value = four[q] if j * q == 0 else times(four[q], 2.0 * math.pi * j * q / RADIX)
            mid[q * 8 + j, :, 0:LANES] = value[0]
            mid[q * 8 + j, :, LANES : 2 * LANES] = value[1]
    for q in range(4):
        eight = dft8(
            [(mid[q * 8 + j, :, 0:LANES], mid[q * 8 + j, :, LANES : 2 * LANES]) for j in range(8)]
        )
        for m in range(8):
            store(q + 4 * m, eight[m])


def forward(load, twist, lane_table, mid, work):
    def store(k, value):
        re, im = value
        c, s = twist[0, pl.ds(k, 1), :], twist[1, pl.ds(k, 1), :]
        work[k, :, 0:LANES] = re * c - im * s
        work[k, :, LANES : 2 * LANES] = re * s + im * c

    dft32(load, mid, store)
    return lanes(work, lane_table)


def lanes(work, lane_table):
    rows = work[...].reshape(RADIX * SUB, 2 * LANES)
    out = jnp.dot(
        rows, lane_table[...], precision=lax.Precision.HIGHEST, preferred_element_type=jnp.float32
    )
    return out.reshape(RADIX, SUB, 2 * LANES)


def inverse(twist, lane_table, mid, work, store):
    work[...] = lanes(work, lane_table)

    def load(k):
        re, im = work[k, :, 0:LANES], work[k, :, LANES : 2 * LANES]
        c, s = twist[0, pl.ds(k, 1), :], twist[1, pl.ds(k, 1), :]
        return re * c - im * s, re * s + im * c

    dft32(load, mid, store)


def kernel(
    n_grp, n_en, rows,
    lesser, greater, mirror, lane_hbm, twist_hbm, out,
    recv_b, recv_a, c_buf, lane_table, twist, spec_b, perm_b, mid, work,
    send_sem, recv_sem, local_sem, self_sem, here_sem, mate_sem,
):
    me_g, me_e = lax.axis_index("grp"), lax.axis_index("en")
    partner = lax.rem(me_g + n_grp // 2, n_grp)
    parts = rows // SUB

    chips = n_en // CORES
    late = jnp.where(lax.rem(me_g, n_grp // 2) == 0, chips - 4, 0)
    me_z = me_e // CORES
    rank = jnp.where(me_z == 0, late, me_z - (me_z <= late).astype(jnp.int32))

    def chip_of(place):
        return jnp.where(place == late, 0, place + (place < late).astype(jnp.int32))

    core = lax.rem(me_e, CORES)
    mates = [(me_g, me_e + 1 - 2 * core), (partner, me_z * CORES), (partner, me_z * CORES + 1)]

    def signal(sem, device):
        pl.semaphore_signal(sem, inc=1, device_id=device, device_id_type=MESH)

    barrier = pltpu.get_barrier_semaphore()
    for mate in mates:
        signal(barrier, mate)

    def greet(place, carry):
        signal(barrier, (me_g, chip_of(place) * CORES + core))
        return carry

    lax.fori_loop(rank + 1, chips, greet, 0)
    pl.semaphore_wait(barrier, rank + len(mates))
    for mate in mates:
        signal(mate_sem, mate)

    def announce(place, carry):
        signal(here_sem.at[rank], (me_g, chip_of(place) * CORES + core))
        return carry

    lax.fori_loop(0, rank, announce, 0)
    pl.semaphore_wait(mate_sem, len(mates))

    def send_b(chip):
        for core in range(CORES):
            other = chip * CORES + core
            pltpu.make_async_remote_copy(
                src_ref=greater.at[:, pl.ds(pl.multiple_of(other * rows, rows), rows), :],
                dst_ref=recv_b.at[me_e],
                send_sem=send_sem.at[0],
                recv_sem=recv_sem.at[0],
                device_id=(partner, other),
                device_id_type=MESH,
            ).start()

    def send_b_below(step, carry):
        send_b(chip_of(lax.rem(rank + chips // 2 + step, rank + 1)))
        return carry

    lax.fori_loop(0, rank + 1, send_b_below, 0)

    def send_b_above(place, carry):
        pl.semaphore_wait(here_sem.at[place], 1)
        send_b(chip_of(place))
        return carry

    lax.fori_loop(rank + 1, chips, send_b_above, 0)

    def order(step):
        turn, kind = (step + 3) // 4, lax.rem(step + 3, 4)
        half = n_en // 2
        hop = jnp.where(
            kind == 0, turn, jnp.where(kind == 1, turn - half, jnp.where(kind == 2, -turn, half - turn))
        )
        hop = jnp.where(step == 0, half, hop)
        return lax.rem(me_e + hop + n_en, n_en)

    flat = lax.rem(me_g // 4, 2)

    def order_wave(step):
        half = n_en // 2
        low = me_e < half
        turn = step // 2
        stay = turn + (turn >= me_e).astype(jnp.int32)
        from_low = jnp.where(lax.rem(step, 2) == 0, half + turn, stay)
        from_high = step + (step >= me_e).astype(jnp.int32)
        return jnp.where(low, from_low, from_high)

    def order_last(step):
        low = me_e < n_en // 2
        mine = jnp.where(low, me_e, n_en - 1 - me_e)
        rest = step - (n_en - 1 - 2 * mine)
        gap = mine - rest // 2
        both = jnp.where(lax.rem(rest, 2) == 0, mine + gap, mine - gap)
        other = jnp.where(rest < 0, n_en - 1 - step, both)
        return jnp.where(low, other, n_en - 1 - other)

    def order_c(step, part):
        calm = order_last(step) if part == parts - 1 else order(step)
        return jnp.where(flat == 1, calm, order_wave(step))

    for part in range(parts):

        def send_a(step, carry, part=part):
            other = jnp.where(flat == 1, order(step), order_wave(step))
            pltpu.make_async_remote_copy(
                src_ref=lesser.at[
                    :, pl.ds(pl.multiple_of(other * rows + part * SUB, SUB), SUB), :
                ],
                dst_ref=recv_a.at[part, me_e],
                send_sem=send_sem.at[1 + part],
                recv_sem=recv_sem.at[1 + part],
                device_id=(me_g, other),
                device_id_type=MESH,
            ).start()
            return carry

        lax.fori_loop(0, n_en - 1, send_a, 0)

    def own(part):
        return pltpu.make_async_copy(
            lesser.at[:, pl.ds(pl.multiple_of(me_e * rows + part * SUB, SUB), SUB), :],
            recv_a.at[part, me_e],
            self_sem.at[part],
        )

    load_lane = pltpu.make_async_copy(lane_hbm, lane_table, local_sem.at[0])
    load_twist = pltpu.make_async_copy(twist_hbm, twist, local_sem.at[1])
    load_lane.start()
    load_twist.start()
    for part in range(parts):
        own(part).start()
    load_lane.wait()
    load_twist.wait()

    def await_recv(ref, sem):
        pltpu.make_async_copy(ref, ref, sem).wait()

    await_recv(recv_b, recv_sem.at[0])
    for part in range(parts):
        spec_b[:, part * SUB : (part + 1) * SUB, :] = forward(
            lambda d, part=part: (
                recv_b[d, 0, part * SUB : (part + 1) * SUB, :],
                recv_b[d, 1, part * SUB : (part + 1) * SUB, :],
            ),
            twist, lane_table, mid, work,
        )
    for row in range(rows):
        pick = lax.rem(mirror[me_e * rows + row], rows)
        perm_b[:, row : row + 1, :] = spec_b[:, pl.ds(pick, 1), :]

    scale = float(RADIX * LANES) ** -1.5
    for part in range(parts):
        own(part).wait()
        await_recv(recv_a.at[part, pl.ds(0, n_en - 1)], recv_sem.at[1 + part])
        spec = forward(
            lambda d, part=part: (recv_a[part, d, 1], recv_a[part, d, 0]),
            twist, lane_table, mid, work,
        )
        left_re, left_im = spec[:, :, 0:LANES], spec[:, :, LANES : 2 * LANES]
        block = perm_b[:, part * SUB : (part + 1) * SUB, :]
        right_re, right_im = block[:, :, 0:LANES], block[:, :, LANES : 2 * LANES]
        work[:, :, 0:LANES] = (left_re * right_re + left_im * right_im) * scale
        work[:, :, LANES : 2 * LANES] = (left_re * right_im - left_im * right_re) * scale

        def store(d, value, part=part):
            c_buf[part, d, 0] = value[0]
            c_buf[part, d, 1] = value[1]

        inverse(twist, lane_table, mid, work, store)

        place = pl.ds(pl.multiple_of(me_e * rows + part * SUB, SUB), SUB)

        def send_c(step, carry, part=part, place=place):
            other = order_c(step, part)
            pltpu.make_async_remote_copy(
                src_ref=c_buf.at[part, other],
                dst_ref=out.at[:, place, :],
                send_sem=send_sem.at[1 + parts + part],
                recv_sem=recv_sem.at[1 + parts],
                device_id=(me_g, other),
                device_id_type=MESH,
            ).start()
            return carry

        lax.fori_loop(0, n_en - 1, send_c, 0)
        pltpu.make_async_copy(
            c_buf.at[part, me_e], out.at[:, place, :], self_sem.at[parts + part]
        ).start()

    for part in range(parts):
        place = pl.ds(pl.multiple_of(me_e * rows + part * SUB, SUB), SUB)
        pltpu.make_async_copy(
            c_buf.at[part, me_e], out.at[:, place, :], self_sem.at[parts + part]
        ).wait()
    await_recv(recv_b, send_sem.at[0])
    for part in range(parts):
        await_recv(recv_a.at[part, pl.ds(0, n_en - 1)], send_sem.at[1 + part])
        await_recv(c_buf.at[part, pl.ds(0, n_en - 1)], send_sem.at[1 + parts + part])
    length = rows * (n_en - 1)
    await_recv(out.at[:, pl.ds(0, length), :], recv_sem.at[1 + parts])


def body(lesser, greater, mirror):
    n_grp, n_en = lax.axis_size("grp"), lax.axis_size("en")
    rows = lesser.shape[1] // n_en
    parts = rows // SUB
    lane_table, twist_table = tables()
    wide = (RADIX, SUB, 2 * LANES)
    f32 = jnp.float32
    return pl.pallas_call(
        functools.partial(kernel, n_grp, n_en, rows),
        out_shape=jax.ShapeDtypeStruct(lesser.shape, f32),
        in_specs=[
            pl.BlockSpec(memory_space=pl.ANY),
            pl.BlockSpec(memory_space=pl.ANY),
            pl.BlockSpec(memory_space=pltpu.SMEM),
            pl.BlockSpec(memory_space=pl.ANY),
            pl.BlockSpec(memory_space=pl.ANY),
        ],
        out_specs=pl.BlockSpec(memory_space=pl.ANY),
        scratch_shapes=[
            pltpu.VMEM((n_en, 2, rows, LANES), f32),
            pltpu.VMEM((parts, n_en, 2, SUB, LANES), f32),
            pltpu.VMEM((parts, n_en, 2, SUB, LANES), f32),
            pltpu.VMEM(lane_table.shape, f32),
            pltpu.VMEM(twist_table.shape, f32),
            pltpu.VMEM((RADIX, rows, 2 * LANES), f32),
            pltpu.VMEM((RADIX, rows, 2 * LANES), f32),
            pltpu.VMEM(wide, f32),
            pltpu.VMEM(wide, f32),
            pltpu.SemaphoreType.DMA((1 + 2 * parts,)),
            pltpu.SemaphoreType.DMA((2 + parts,)),
            pltpu.SemaphoreType.DMA((2,)),
            pltpu.SemaphoreType.DMA((2 * parts,)),
            pltpu.SemaphoreType.REGULAR((n_en // CORES,)),
            pltpu.SemaphoreType.REGULAR,
        ],
        compiler_params=pltpu.CompilerParams(
            collective_id=0, has_side_effects=True, vmem_limit_bytes=60 * 1024 * 1024
        ),
    )(lesser, greater, mirror, jnp.asarray(lane_table), jnp.asarray(twist_table))


def solution(mesh):
    in_specs = (P(None, "grp", "en"), P(None, "grp", "en"), P("grp"))
    out_specs = P(None, "grp", "en")
    return jax.shard_map(body, mesh=mesh, in_specs=in_specs, out_specs=out_specs, check_vma=False)
```

```python
import functools
import math

import jax
import jax.numpy as jnp
import numpy as np
from jax import lax
from jax.experimental import pallas as pl
from jax.experimental.pallas import tpu as pltpu
from jax.sharding import PartitionSpec as P

MESH = pl.DeviceIdType.MESH
RADIX = 32
LANES = 128
SUB = 8
CORES = 2


def tables():
    length = RADIX * LANES
    lane = np.arange(LANES)
    angle = 2.0 * math.pi / LANES * (lane[:, None] * lane[None, :] % LANES)
    cos, sin = np.cos(angle), np.sin(angle)
    lane_table = np.block([[cos, sin], [-sin, cos]]).astype(np.float32)
    series = np.arange(RADIX)
    twist = 2.0 * math.pi / length * (series[:, None] * lane[None, :] % length)
    twist_table = np.stack([np.cos(twist), np.sin(twist)]).astype(np.float32)
    return lane_table, twist_table


def times(value, turn):
    re, im = value
    c, s = math.cos(turn), math.sin(turn)
    return re * c - im * s, re * s + im * c


def add(left, right):
    return left[0] + right[0], left[1] + right[1]


def sub(left, right):
    return left[0] - right[0], left[1] - right[1]


def quarter(value):
    return -value[1], value[0]


def dft4(x):
    s02, d02 = add(x[0], x[2]), sub(x[0], x[2])
    s13, d13 = add(x[1], x[3]), quarter(sub(x[1], x[3]))
    return [add(s02, s13), add(d02, d13), sub(s02, s13), sub(d02, d13)]


def dft8(x):
    even, odd = dft4(x[0::2]), dft4(x[1::2])
    root = math.sqrt(0.5)
    r1, i1 = odd[1]
    odd[1] = ((r1 - i1) * root, (r1 + i1) * root)
    odd[2] = quarter(odd[2])
    r3, i3 = odd[3]
    odd[3] = ((-r3 - i3) * root, (r3 - i3) * root)
    return [add(e, o) for e, o in zip(even, odd)] + [sub(e, o) for e, o in zip(even, odd)]


def dft32(load, mid, store):
    for j in range(8):
        four = dft4([load(8 * i + j) for i in range(4)])
        for q in range(4):
            value = four[q] if j * q == 0 else times(four[q], 2.0 * math.pi * j * q / RADIX)
            mid[q * 8 + j, :, 0:LANES] = value[0]
            mid[q * 8 + j, :, LANES : 2 * LANES] = value[1]
    for q in range(4):
        eight = dft8(
            [(mid[q * 8 + j, :, 0:LANES], mid[q * 8 + j, :, LANES : 2 * LANES]) for j in range(8)]
        )
        for m in range(8):
            store(q + 4 * m, eight[m])


def forward(load, twist, lane_table, mid, work):
    def store(k, value):
        re, im = value
        c, s = twist[0, pl.ds(k, 1), :], twist[1, pl.ds(k, 1), :]
        work[k, :, 0:LANES] = re * c - im * s
        work[k, :, LANES : 2 * LANES] = re * s + im * c

    dft32(load, mid, store)
    return lanes(work, lane_table)


def lanes(work, lane_table):
    rows = work[...].reshape(RADIX * SUB, 2 * LANES)
    out = jnp.dot(
        rows, lane_table[...], precision=lax.Precision.HIGHEST, preferred_element_type=jnp.float32
    )
    return out.reshape(RADIX, SUB, 2 * LANES)


def inverse(twist, lane_table, mid, work, store):
    work[...] = lanes(work, lane_table)

    def load(k):
        re, im = work[k, :, 0:LANES], work[k, :, LANES : 2 * LANES]
        c, s = twist[0, pl.ds(k, 1), :], twist[1, pl.ds(k, 1), :]
        return re * c - im * s, re * s + im * c

    dft32(load, mid, store)


def kernel(
    n_grp, n_en, rows,
    lesser, greater, mirror, lane_hbm, twist_hbm, out,
    recv_b, recv_a, c_buf, lane_table, twist, spec_b, perm_b, mid, work,
    send_sem, recv_sem, local_sem, self_sem, here_sem, mate_sem,
):
    me_g, me_e = lax.axis_index("grp"), lax.axis_index("en")
    partner = lax.rem(me_g + n_grp // 2, n_grp)
    parts = rows // SUB

    chips = n_en // CORES
    late = jnp.where(lax.rem(me_g, n_grp // 2) == 0, chips - 4, 0)
    me_z = me_e // CORES
    rank = jnp.where(me_z == 0, late, me_z - (me_z <= late).astype(jnp.int32))

    def chip_of(place):
        return jnp.where(place == late, 0, place + (place < late).astype(jnp.int32))

    core = lax.rem(me_e, CORES)
    mates = [(me_g, me_e + 1 - 2 * core), (partner, me_z * CORES), (partner, me_z * CORES + 1)]

    def signal(sem, device):
        pl.semaphore_signal(sem, inc=1, device_id=device, device_id_type=MESH)

    barrier = pltpu.get_barrier_semaphore()
    for mate in mates:
        signal(barrier, mate)

    def greet(place, carry):
        signal(barrier, (me_g, chip_of(place) * CORES + core))
        return carry

    lax.fori_loop(rank + 1, chips, greet, 0)
    pl.semaphore_wait(barrier, rank + len(mates))
    for mate in mates:
        signal(mate_sem, mate)

    def announce(place, carry):
        signal(here_sem.at[rank], (me_g, chip_of(rank - 1 - place) * CORES + core))
        return carry

    lax.fori_loop(0, rank, announce, 0)
    pl.semaphore_wait(mate_sem, len(mates))

    def send_b(chip):
        for core in range(CORES):
            other = chip * CORES + core
            pltpu.make_async_remote_copy(
                src_ref=greater.at[:, pl.ds(pl.multiple_of(other * rows, rows), rows), :],
                dst_ref=recv_b.at[me_e],
                send_sem=send_sem.at[0],
                recv_sem=recv_sem.at[0],
                device_id=(partner, other),
                device_id_type=MESH,
            ).start()

    def send_b_below(step, carry):
        send_b(chip_of(lax.rem(rank + chips // 2 + step, rank + 1)))
        return carry

    lax.fori_loop(0, rank + 1, send_b_below, 0)

    def send_b_above(place, carry):
        pl.semaphore_wait(here_sem.at[place], 1)
        send_b(chip_of(place))
        return carry

    lax.fori_loop(rank + 1, chips, send_b_above, 0)

    def order(step):
        turn, kind = (step + 3) // 4, lax.rem(step + 3, 4)
        half = n_en // 2
        hop = jnp.where(
            kind == 0, turn, jnp.where(kind == 1, turn - half, jnp.where(kind == 2, -turn, half - turn))
        )
        hop = jnp.where(step == 0, half, hop)
        return lax.rem(me_e + hop + n_en, n_en)

    flat = lax.rem(me_g // 4, 2)

    def order_wave(step):
        half = n_en // 2
        low = me_e < half
        turn = step // 2
        stay = turn + (turn >= me_e).astype(jnp.int32)
        from_low = jnp.where(lax.rem(step, 2) == 0, half + turn, stay)
        from_high = step + (step >= me_e).astype(jnp.int32)
        return jnp.where(low, from_low, from_high)

    def order_last(step):
        low = me_e < n_en // 2
        mine = jnp.where(low, me_e, n_en - 1 - me_e)
        rest = step - (n_en - 1 - 2 * mine)
        gap = mine - rest // 2
        both = jnp.where(lax.rem(rest, 2) == 0, mine + gap, mine - gap)
        other = jnp.where(rest < 0, n_en - 1 - step, both)
        return jnp.where(low, other, n_en - 1 - other)

    def order_c(step, part):
        calm = order_last(step) if part == parts - 1 else order(step)
        return jnp.where(flat == 1, calm, order_wave(step))

    for part in range(parts):

        def send_a(step, carry, part=part):
            other = jnp.where(flat == 1, order(step), order_wave(step))
            pltpu.make_async_remote_copy(
                src_ref=lesser.at[
                    :, pl.ds(pl.multiple_of(other * rows + part * SUB, SUB), SUB), :
                ],
                dst_ref=recv_a.at[part, me_e],
                send_sem=send_sem.at[1 + part],
                recv_sem=recv_sem.at[1 + part],
                device_id=(me_g, other),
                device_id_type=MESH,
            ).start()
            return carry

        lax.fori_loop(0, n_en - 1, send_a, 0)

    def own(part):
        return pltpu.make_async_copy(
            lesser.at[:, pl.ds(pl.multiple_of(me_e * rows + part * SUB, SUB), SUB), :],
            recv_a.at[part, me_e],
            self_sem.at[part],
        )

    load_lane = pltpu.make_async_copy(lane_hbm, lane_table, local_sem.at[0])
    load_twist = pltpu.make_async_copy(twist_hbm, twist, local_sem.at[1])
    load_lane.start()
    load_twist.start()
    for part in range(parts):
        own(part).start()
    load_lane.wait()
    load_twist.wait()

    def await_recv(ref, sem):
        pltpu.make_async_copy(ref, ref, sem).wait()

    await_recv(recv_b, recv_sem.at[0])
    for part in range(parts):
        spec_b[:, part * SUB : (part + 1) * SUB, :] = forward(
            lambda d, part=part: (
                recv_b[d, 0, part * SUB : (part + 1) * SUB, :],
                recv_b[d, 1, part * SUB : (part + 1) * SUB, :],
            ),
            twist, lane_table, mid, work,
        )
    for row in range(rows):
        pick = lax.rem(mirror[me_e * rows + row], rows)
        perm_b[:, row : row + 1, :] = spec_b[:, pl.ds(pick, 1), :]

    scale = float(RADIX * LANES) ** -1.5
    for part in range(parts):
        own(part).wait()
        await_recv(recv_a.at[part, pl.ds(0, n_en - 1)], recv_sem.at[1 + part])
        spec = forward(
            lambda d, part=part: (recv_a[part, d, 1], recv_a[part, d, 0]),
            twist, lane_table, mid, work,
        )
        left_re, left_im = spec[:, :, 0:LANES], spec[:, :, LANES : 2 * LANES]
        block = perm_b[:, part * SUB : (part + 1) * SUB, :]
        right_re, right_im = block[:, :, 0:LANES], block[:, :, LANES : 2 * LANES]
        work[:, :, 0:LANES] = (left_re * right_re + left_im * right_im) * scale
        work[:, :, LANES : 2 * LANES] = (left_re * right_im - left_im * right_re) * scale

        def store(d, value, part=part):
            c_buf[part, d, 0] = value[0]
            c_buf[part, d, 1] = value[1]

        inverse(twist, lane_table, mid, work, store)

        place = pl.ds(pl.multiple_of(me_e * rows + part * SUB, SUB), SUB)

        def send_c(step, carry, part=part, place=place):
            other = order_c(step, part)
            pltpu.make_async_remote_copy(
                src_ref=c_buf.at[part, other],
                dst_ref=out.at[:, place, :],
                send_sem=send_sem.at[1 + parts + part],
                recv_sem=recv_sem.at[1 + parts],
                device_id=(me_g, other),
                device_id_type=MESH,
            ).start()
            return carry

        lax.fori_loop(0, n_en - 1, send_c, 0)
        pltpu.make_async_copy(
            c_buf.at[part, me_e], out.at[:, place, :], self_sem.at[parts + part]
        ).start()

    for part in range(parts):
        place = pl.ds(pl.multiple_of(me_e * rows + part * SUB, SUB), SUB)
        pltpu.make_async_copy(
            c_buf.at[part, me_e], out.at[:, place, :], self_sem.at[parts + part]
        ).wait()
    await_recv(recv_b, send_sem.at[0])
    for part in range(parts):
        await_recv(recv_a.at[part, pl.ds(0, n_en - 1)], send_sem.at[1 + part])
        await_recv(c_buf.at[part, pl.ds(0, n_en - 1)], send_sem.at[1 + parts + part])
    length = rows * (n_en - 1)
    await_recv(out.at[:, pl.ds(0, length), :], recv_sem.at[1 + parts])


def body(lesser, greater, mirror):
    n_grp, n_en = lax.axis_size("grp"), lax.axis_size("en")
    rows = lesser.shape[1] // n_en
    parts = rows // SUB
    lane_table, twist_table = tables()
    wide = (RADIX, SUB, 2 * LANES)
    f32 = jnp.float32
    return pl.pallas_call(
        functools.partial(kernel, n_grp, n_en, rows),
        out_shape=jax.ShapeDtypeStruct(lesser.shape, f32),
        in_specs=[
            pl.BlockSpec(memory_space=pl.ANY),
            pl.BlockSpec(memory_space=pl.ANY),
            pl.BlockSpec(memory_space=pltpu.SMEM),
            pl.BlockSpec(memory_space=pl.ANY),
            pl.BlockSpec(memory_space=pl.ANY),
        ],
        out_specs=pl.BlockSpec(memory_space=pl.ANY),
        scratch_shapes=[
            pltpu.VMEM((n_en, 2, rows, LANES), f32),
            pltpu.VMEM((parts, n_en, 2, SUB, LANES), f32),
            pltpu.VMEM((parts, n_en, 2, SUB, LANES), f32),
            pltpu.VMEM(lane_table.shape, f32),
            pltpu.VMEM(twist_table.shape, f32),
            pltpu.VMEM((RADIX, rows, 2 * LANES), f32),
            pltpu.VMEM((RADIX, rows, 2 * LANES), f32),
            pltpu.VMEM(wide, f32),
            pltpu.VMEM(wide, f32),
            pltpu.SemaphoreType.DMA((1 + 2 * parts,)),
            pltpu.SemaphoreType.DMA((2 + parts,)),
            pltpu.SemaphoreType.DMA((2,)),
            pltpu.SemaphoreType.DMA((2 * parts,)),
            pltpu.SemaphoreType.REGULAR((n_en // CORES,)),
            pltpu.SemaphoreType.REGULAR,
        ],
        compiler_params=pltpu.CompilerParams(
            collective_id=0, has_side_effects=True, vmem_limit_bytes=60 * 1024 * 1024
        ),
    )(lesser, greater, mirror, jnp.asarray(lane_table), jnp.asarray(twist_table))


def solution(mesh):
    in_specs = (P(None, "grp", "en"), P(None, "grp", "en"), P("grp"))
    out_specs = P(None, "grp", "en")
    return jax.shard_map(body, mesh=mesh, in_specs=in_specs, out_specs=out_specs, check_vma=False)
```
